32 devices in a mesh: parts: 2 (over y), row: 4 (over x, core), col: 4 (over z).
Axes of the slice: x: 2, y: 2, z: 4, core: 2. Of those that a mesh axis runs over, the one named last changes fastest.
Arguments:
- left_factor: bfloat16 [6144, 8, 1024], P(('parts', 'col'), None, 'row'), parts along dimension 0, may hold values from -0.109375 to 0.109375
- right_factor: bfloat16 [64, 1024, 3072], P('parts', 'col', 'row'), parts along dimension 0, may hold values from -6 to 6
- amplitudes: bfloat16 [1024, 1024, 512], P('row', 'col', 'parts'), parts along dimension 2, may hold values from -0.0078125 to 0.0078125
Outputs:
- ladder: float32 [512, 256], P(('parts', 'row', 'col')), parts along dimension 0
The draws below stay inside these ranges and needn't reach their ends.
There are 2 independent parts, one for each index of `parts`. The reference program is written for one: setup_inputs(seed, part) draws one part's arguments, and reference() takes and returns one part's arrays. A program takes and returns all parts, laid end to end along the dimension named above; each array names one. Nothing has to cross between parts.
All inputs are finite; a program needn't handle non-finite values.
Results may differ from the reference program's by a relative error of at most 0.0029.
Values may be sent and summed in bfloat16 or wider, within the bound.
No kernel may reach another device: no remote copies, remote signals or barrier semaphores. Data moves between devices by JAX's collectives and lax.ppermute only.
A program may use at most 192 MiB of HBM per device.

```python
import jax
import jax.numpy as jnp
from jax import lax

V = 1024
NAUX = 3072
NA = 8
NB = 32
P_SIZE = 256


def strengthened(array, key, source, target, parts, factor):
    def block_of(position):
        return (jnp.arange(array.shape[position]) // (array.shape[position] // parts)).reshape((-1,) + (1,) * (array.ndim - 1 - position))

    near = jax.random.permutation(key, parts)[block_of(target)]
    second = (block_of(target) + parts // 2) % parts
    return jnp.where((block_of(source) == near) | (block_of(source) == second), factor * array, array)


def shard_levels(key, dims, cuts, low, top_value):
    gain = 1.0
    for axis_at, shards_of in cuts:
        steps = jax.random.uniform(jax.random.fold_in(jax.random.fold_in(key, 6), axis_at), (shards_of,), jnp.float32, low / len(cuts), top_value / len(cuts))
        gain = gain * jnp.repeat(jnp.exp(steps), dims[axis_at] // shards_of).reshape((-1,) + (1,) * (len(dims) - 1 - axis_at))
    return gain


def gaussian(key, shape, scale, most, pieces=(), dtype=jnp.bfloat16):
    array = jax.random.normal(key, shape, jnp.float32) * scale
    if len(pieces) > 0:
        array = shard_levels(key, shape, pieces, -0.22, 0.18) * array
    return jnp.clip(array, min=-most, max=most).astype(dtype)


def heavy_noise(rng, extent, spread, most, shards, heavy, dtype=jnp.bfloat16):
    values = spread * jax.random.normal(rng, extent, jnp.float32)
    if shards:
        values = values * shard_levels(rng, extent, shards, -0.22, 0.18)
    return jnp.clip(strengthened(values, jax.random.fold_in(rng, 3), *heavy), -most, most).astype(dtype)


def setup_inputs(seed: int = 0, part: int = 0) -> dict:
    seeds = jax.random.split(jax.random.key(seed), 4)
    own_keys = jax.random.split(jax.random.fold_in(seeds[3], part), 4)
    return {
        "left_factor": gaussian(own_keys[0], (NAUX, NA, V), NAUX ** -0.5, 0.109375, ((0, 4), (2, 4))),
        "right_factor": gaussian(own_keys[1], (NB, V, NAUX), 1.0, 6.0, ((1, 4), (2, 4))),
        "amplitudes": heavy_noise(own_keys[2], (V, V, P_SIZE), (V * V) ** -0.5, 0.0078125, ((0, 4), (1, 4)), (1, 2, 4, 2.0)),
    }


def reference(left_factor, right_factor, amplitudes):
    right_flat = right_factor.reshape(NB * V, NAUX)
    amp_flat = amplitudes.reshape(V * V, P_SIZE)

    def one_virtual(left_slice):
        integral = lax.dot_general(left_slice, right_flat, (((0,), (1,)), ((), ())), preferred_element_type=jnp.float32).astype(jnp.bfloat16)
        ordered = integral.reshape(V, NB, V).transpose(0, 2, 1).reshape(V * V, NB)
        return lax.dot_general(amp_flat, ordered, (((0,), (0,)), ((), ())), preferred_element_type=jnp.float32)

    stacked = lax.map(one_virtual, jnp.moveaxis(left_factor, 1, 0))
    return jnp.transpose(stacked, (1, 0, 2)).reshape(P_SIZE, NA * NB)
```

```python
import functools
import math

import jax
import jax.numpy as jnp
from jax import lax
from jax.experimental import pallas as pl
from jax.experimental.pallas import tpu as pltpu
from jax.sharding import PartitionSpec as P

CHUNK_SHARES = (2, 4, 2, 3, 3, 2)
PIECES = ((0, 8, 0), (0, 4, 1), (4, 4, 1))


def ladder_kernel(place_ref, total_ref, amp_ref, *refs, pieces, chunk_steps, ranks, first_step, span):
    count_l, count_r = len(pieces), len(chunk_steps) * ranks
    left_refs, right_refs = refs[:count_l], refs[count_l : count_l + count_r]
    out_ref = refs[count_l + count_r]
    rest = refs[count_l + count_r + 1 :]
    left_bufs = rest[:count_l]
    right_buf, amp_buf, integral_ref, left_sem, right_sem, amp_sem = rest[count_l:]
    _, _, step_d, width_b, depth = right_buf.shape
    steps = sum(chunk_steps)
    halves = sorted({half for _, _, half in pieces})
    low_c, wide_c = halves[0] * span, len(halves) * span
    step = pl.program_id(0)
    slot = lax.rem(step, 2)
    place = place_ref[0]

    def left_copy(k, a, m):
        rows = pl.ds(pl.multiple_of((place ^ m) * depth, depth), depth)
        columns = pl.ds(a * span, min(pieces[k][1], 4) * span)
        return pltpu.make_async_copy(
            left_refs[k].at[rows, columns], left_bufs[k].at[rows, columns], left_sem.at[k, a // 4, m]
        )

    def right_copy(j, offset, to, m):
        source = right_refs[j * ranks + m].at[pl.ds(offset * step_d, step_d)]
        return pltpu.make_async_copy(source, right_buf.at[to, m], right_sem.at[to, m])

    def amp_copy(at, to):
        rows = pl.ds((first_step + at) * step_d, step_d)
        return pltpu.make_async_copy(
            amp_ref.at[rows, pl.ds(low_c, wide_c)], amp_buf.at[to], amp_sem.at[to]
        )

    def fetch_right(at, to):
        begin = 0
        for j, n in enumerate(chunk_steps):

            @pl.when((at >= begin) & (at < begin + n))
            def _():
                for m in range(ranks):
                    right_copy(j, at - begin, to, m).start()

            begin += n

    def integrals(to, first):
        row = 0
        for k, (_, count, _) in enumerate(pieces):
            wide = min(count, 4)
            for a in range(0, count, wide):
                product = None
                for m in range(ranks):
                    if first and k == 0 and a == 0:
                        right_copy(0, 0, to, m).wait()
                    if first:
                        left_copy(k, a, m).wait()
                    start = pl.multiple_of((place ^ m) * depth, depth)
                    term = jnp.dot(
                        right_buf[to, m].reshape(step_d * width_b, depth),
                        left_bufs[k][pl.ds(start, depth), a * span : (a + wide) * span],
                        preferred_element_type=jnp.float32,
                    )
                    product = term if product is None else product + term
                rounded = product.astype(jnp.bfloat16)
                for i in range(wide):
                    for d in range(step_d):
                        integral_ref[to, row : row + width_b, d * span : (d + 1) * span] = rounded[
                            d * width_b : (d + 1) * width_b, i * span : (i + 1) * span
                        ]
                    row += width_b

    def ladder(at):
        row = 0
        for first, count, half in pieces:
            low = halves.index(half) * span
            weights = amp_buf[at, :, low : low + span, :].reshape(step_d * span, amp_buf.shape[3])
            size = count * width_b
            out_ref[first * width_b : first * width_b + size, :] += jnp.dot(
                integral_ref[at, row : row + size, :], weights, preferred_element_type=jnp.float32
            )
            row += size

    @pl.when(step == 0)
    def _():
        for k, (_, count, _) in enumerate(pieces):
            for a in range(0, count, 4):
                for m in range(ranks):
                    if k == 0 and a == 0:
                        right_copy(0, 0, 0, m).start()
                    left_copy(k, a, m).start()
        out_ref[...] = total_ref[...]

    amp_copy(step, slot).start()
    if steps > 1:

        @pl.when(step + 1 < steps)
        def _():
            fetch_right(step + 1, 1 - slot)

    @pl.when(step == 0)
    def _():
        integrals(0, True)

    if steps > 1:

        @pl.when(step > 0)
        def _():
            for m in range(ranks):
                right_copy(0, 0, slot, m).wait()
            amp_copy(0, 1 - slot).wait()
            ladder(1 - slot)
            integrals(slot, False)

    @pl.when(step == steps - 1)
    def _():
        amp_copy(0, slot).wait()
        ladder(slot)


def add_ladder(place, total, amp, first_d, span, lefts, rights, pieces, step_d):
    _, width_b, depth = rights[0][0].shape
    ranks = len(rights[0])
    pair_count = amp.shape[2]
    chunk_steps = tuple(blocks[0].shape[0] // step_d for blocks in rights)
    steps = sum(chunk_steps)
    halves = {half for _, _, half in pieces}
    count_a = sum(count for _, count, _ in pieces)
    columns = count_a * span
    flops = 2 * steps * step_d * width_b * columns * (depth * ranks + pair_count)
    blocks = [block for chunk in rights for block in chunk]
    anywhere = pl.BlockSpec(memory_space=pl.ANY)
    return pl.pallas_call(
        functools.partial(
            ladder_kernel,
            pieces=pieces,
            chunk_steps=chunk_steps,
            ranks=ranks,
            first_step=first_d // step_d,
            span=span,
        ),
        out_shape=jax.ShapeDtypeStruct(total.shape, total.dtype),
        grid_spec=pltpu.PrefetchScalarGridSpec(
            num_scalar_prefetch=1,
            grid=(steps,),
            in_specs=[pl.BlockSpec(total.shape, lambda s, _: (0, 0))]
            + [anywhere] * (1 + len(lefts) + len(blocks)),
            out_specs=pl.BlockSpec(total.shape, lambda s, _: (0, 0)),
            scratch_shapes=[pltpu.VMEM(x.shape, x.dtype) for x in lefts]
            + [
                pltpu.VMEM((2, ranks, step_d, width_b, depth), jnp.bfloat16),
                pltpu.VMEM((2, step_d, span * len(halves), pair_count), jnp.bfloat16),
                pltpu.VMEM((2, count_a * width_b, step_d * span), jnp.bfloat16),
                pltpu.SemaphoreType.DMA((len(lefts), -(-max(n for _, n, _ in pieces) // 4), ranks)),
                pltpu.SemaphoreType.DMA((2, ranks)),
                pltpu.SemaphoreType.DMA((2,)),
            ],
        ),
        input_output_aliases={1: 0},
        compiler_params=pltpu.CompilerParams(vmem_limit_bytes=VMEM_BYTES),
        cost_estimate=pl.CostEstimate(
            flops=flops // 20,
            bytes_accessed=2 * depth * ranks * (columns + steps * step_d * width_b),
            transcendentals=0,
        ),
    )(place, total, amp, *lefts, *blocks)


VMEM_BYTES = 62 * 2**20
SMALL_COST = pl.CostEstimate(flops=0, bytes_accessed=2**16, transcendentals=0)


def turn_kernel(in_ref, out_ref, wide_ref):
    outer, inner, width = in_ref.shape
    for k in range(width // 128):
        lanes = slice(k * 128, (k + 1) * 128)
        wide_ref[k] = in_ref[:, :, lanes].astype(jnp.float32).reshape(outer * inner, 128)
        for i in range(inner):
            out_ref[i, :, lanes] = wide_ref[k, pl.ds(i, outer, stride=inner), :].astype(out_ref.dtype)


def turn(array, start, size):
    outer, _, width = array.shape
    inner = 16
    if start % inner or size % inner or width % 128 or outer % 16:
        return jnp.transpose(array[:, start : start + size], (1, 0, 2))
    block = math.gcd(outer, 64)
    return pl.pallas_call(
        turn_kernel,
        out_shape=jax.ShapeDtypeStruct((size, outer, width), array.dtype),
        grid=(size // inner, outer // block),
        in_specs=[pl.BlockSpec((block, inner, width), lambda i, j: (j, start // inner + i, 0))],
        out_specs=pl.BlockSpec((inner, block, width), lambda i, j: (i, j, 0)),
        scratch_shapes=[pltpu.VMEM((width // 128, block * inner, 128), jnp.float32)],
        compiler_params=pltpu.CompilerParams(vmem_limit_bytes=VMEM_BYTES),
        cost_estimate=SMALL_COST,
    )(array)


def split_kernel(in_ref, *refs, pieces, span):
    wide_ref = refs[-1]
    rows, count_a, _ = in_ref.shape
    for half in sorted({half for _, _, half in pieces}):
        lanes = slice(half * span, (half + 1) * span)
        wide_ref[half] = in_ref[:, :, lanes].astype(jnp.float32).reshape(rows * count_a, span)
    for (first, count, half), out_ref in zip(pieces, refs):
        for a in range(count):
            picked = wide_ref[half, pl.ds(first + a, rows, stride=count_a), :]
            out_ref[:, a * span : (a + 1) * span] = picked.astype(out_ref.dtype)


def split_left(array, pieces, span):
    rows, count_a, span_c = array.shape
    block = math.gcd(rows, 256)
    return pl.pallas_call(
        functools.partial(split_kernel, pieces=pieces, span=span),
        out_shape=[jax.ShapeDtypeStruct((rows, count * span), array.dtype) for _, count, _ in pieces],
        grid=(rows // block,),
        in_specs=[pl.BlockSpec((block, count_a, span_c), lambda i: (i, 0, 0))],
        out_specs=[pl.BlockSpec((block, count * span), lambda i: (i, 0)) for _, count, _ in pieces],
        scratch_shapes=[pltpu.VMEM((span_c // span, block * count_a, span), jnp.float32)],
        compiler_params=pltpu.CompilerParams(vmem_limit_bytes=VMEM_BYTES),
        cost_estimate=SMALL_COST,
    )(array)


def swap(block, axis, bit, size):
    return lax.ppermute(block, axis, [(i, i ^ bit) for i in range(size)])


def scatter_sum(total, axis, size):
    place = lax.axis_index(axis)
    if size <= 4:
        rows = total.shape[0] // size

        def share(owner):
            return lax.dynamic_slice_in_dim(total, owner * rows, rows, 0)

        gives = [share(place ^ mask) for mask in range(1, size)]
        return sum([swap(give, axis, m + 1, size) for m, give in enumerate(gives)], share(place))
    bit = size // 2
    while bit:
        rows = total.shape[0] // 2
        mine = (place // bit) % 2
        keep = lax.dynamic_slice_in_dim(total, mine * rows, rows, 0)
        give = lax.dynamic_slice_in_dim(total, (1 - mine) * rows, rows, 0)
        total = keep + swap(give, axis, bit, size)
        bit //= 2
    return total


def on_device(left_factor, right_factor, amplitudes, *, row_size, col_size):
    width_a = left_factor.shape[1]
    span_c = left_factor.shape[2]
    width_b, span_d, depth = right_factor.shape
    pair_count = amplitudes.shape[2]
    span = span_c // 2
    place = lax.axis_index("row").astype(jnp.int32).reshape(1)

    pieces = [(f * width_a // 8, n * width_a // 8, h) for f, n, h in PIECES]

    chunks = [share * span_d // 16 for share in CHUNK_SHARES]
    starts = [sum(chunks[:j]) for j in range(len(chunks))]
    step_d = math.gcd(16, *chunks)

    together = lax.optimization_barrier
    far_bit = row_size // 2
    near_bits = [1 << k for k in reversed(range(row_size.bit_length() - 2))]

    def spread(held):
        for bit in near_bits:
            held = held | {m ^ bit: swap(x, "row", bit, row_size) for m, x in held.items()}
        return held

    parts = split_left(left_factor, pieces, span)
    parts, right_factor = together((parts, right_factor))
    owns = [turn(right_factor, starts[0], chunks[0])]
    owns[0], right_factor = together((owns[0], right_factor))

    by_hand = col_size == 4
    lefts = [lax.all_gather(part, "col", axis=0, tiled=True) for part in (parts[:-1] if by_hand else parts)]
    round_trip = [parts[-1]]
    around = [(i, (i + 1) % col_size) for i in range(col_size)]

    total = jnp.zeros((width_a * width_b, pair_count), jnp.float32)
    rights = [spread({0: owns[0]})]
    for j, calls in enumerate(STAGES):
        moving = j < len(chunks)
        if moving:
            far = swap(owns[j], "row", far_bit, row_size)
        if by_hand and j + 1 < col_size:
            round_trip.append(lax.ppermute(round_trip[-1], "col", around))
        if j == 0:
            owns.append(turn(right_factor, starts[1], chunks[1]))
        if j == 1:
            owns += [turn(right_factor, s, n) for s, n in zip(starts[2:], chunks[2:])]
            owns, amplitudes = together((owns, amplitudes))
            amp = jnp.transpose(amplitudes, (1, 0, 2))
        if by_hand and j + 1 == col_size:
            rows = round_trip[0].shape[0]
            here = lax.axis_index("col")
            joined = jnp.zeros((col_size * rows, round_trip[0].shape[1]), round_trip[0].dtype)
            for hop, block in enumerate(round_trip):
                owner = lax.rem(here - hop + col_size, col_size)
                joined = lax.dynamic_update_slice_in_dim(joined, block, owner * rows, 0)
            lefts.append(joined)
        for chosen, js in calls:
            total = add_ladder(
                place, total, amp, starts[js[0]], span,
                [lefts[k] for k in chosen],
                [[rights[i][m] for m in range(row_size)] for i in js],
                [pieces[k] for k in chosen], step_d,
            )
        if moving:
            if j == 0:
                far, total, owns, round_trip, right_factor, amplitudes = together(
                    (far, total, owns, round_trip, right_factor, amplitudes)
                )
            elif j + 1 < col_size:
                far, total, owns, round_trip, amp = together((far, total, owns, round_trip, amp))
            else:
                far, total, owns = together((far, total, owns))
            rights[j] |= spread({far_bit: far})
            if j + 1 < len(chunks):
                rights.append(spread({0: owns[j + 1]}))
    total = scatter_sum(total.T, "row", row_size)
    return scatter_sum(total, "col", col_size)


STAGES = (
    (),
    (),
    (),
    (((2,), (0, 1)), ((0,), (0, 1, 2))),
    (((2,), (2,)), ((0, 2), (3,)), ((1,), (0, 1, 2))),
    (((1,), (3,)), ((0, 2), (4,))),
    (((1,), (4,)), ((0, 1, 2), (5,))),
)


def solution(mesh):
    return jax.shard_map(
        functools.partial(on_device, row_size=mesh.shape["row"], col_size=mesh.shape["col"]),
        mesh=mesh,
        in_specs=(
            P(("parts", "col"), None, "row"),
            P("parts", "col", "row"),
            P("row", "col", "parts"),
        ),
        out_specs=P(("parts", "row", "col"), None),
        check_vma=False,
    )
```

```python
import functools
import math

import jax
import jax.numpy as jnp
from jax import lax
from jax.experimental import pallas as pl
from jax.experimental.pallas import tpu as pltpu
from jax.sharding import PartitionSpec as P

CHUNK_SHARES = (3, 4, 3, 2, 2, 2)
PIECES = ((0, 8, 0), (0, 4, 1), (4, 4, 1))


def ladder_kernel(place_ref, total_ref, amp_ref, *refs, pieces, chunk_steps, ranks, first_step, span):
    count_l, count_r = len(pieces), len(chunk_steps) * ranks
    left_refs, right_refs = refs[:count_l], refs[count_l : count_l + count_r]
    out_ref = refs[count_l + count_r]
    rest = refs[count_l + count_r + 1 :]
    left_bufs = rest[:count_l]
    right_buf, amp_buf, integral_ref, left_sem, right_sem, amp_sem = rest[count_l:]
    _, _, step_d, width_b, depth = right_buf.shape
    steps = sum(chunk_steps)
    halves = sorted({half for _, _, half in pieces})
    low_c, wide_c = halves[0] * span, len(halves) * span
    step = pl.program_id(0)
    slot = lax.rem(step, 2)
    place = place_ref[0]

    def left_copy(k, a):
        columns = pl.ds(a * span, min(pieces[k][1], 4) * span)
        return pltpu.make_async_copy(
            left_refs[k].at[:, columns], left_bufs[k].at[:, columns], left_sem.at[k, a // 4]
        )

    def right_copy(j, offset, to, m):
        source = right_refs[j * ranks + m].at[pl.ds(offset * step_d, step_d)]
        return pltpu.make_async_copy(source, right_buf.at[to, m], right_sem.at[to, m])

    def amp_copy(at, to):
        rows = pl.ds((first_step + at) * step_d, step_d)
        return pltpu.make_async_copy(
            amp_ref.at[rows, pl.ds(low_c, wide_c)], amp_buf.at[to], amp_sem.at[to]
        )

    def fetch_right(at, to):
        begin = 0
        for j, n in enumerate(chunk_steps):

            @pl.when((at >= begin) & (at < begin + n))
            def _():
                for m in range(ranks):
                    right_copy(j, at - begin, to, m).start()

            begin += n

    def integrals(to, first):
        row = 0
        for k, (_, count, _) in enumerate(pieces):
            wide = min(count, 4)
            for a in range(0, count, wide):
                if first:
                    left_copy(k, a).wait()
                product = None
                for m in range(ranks):
                    start = pl.multiple_of((place ^ m) * depth, depth)
                    term = jnp.dot(
                        right_buf[to, m].reshape(step_d * width_b, depth),
                        left_bufs[k][pl.ds(start, depth), a * span : (a + wide) * span],
                        preferred_element_type=jnp.float32,
                    )
                    product = term if product is None else product + term
                rounded = product.astype(jnp.bfloat16)
                for i in range(wide):
                    for d in range(step_d):
                        integral_ref[to, row : row + width_b, d * span : (d + 1) * span] = rounded[
                            d * width_b : (d + 1) * width_b, i * span : (i + 1) * span
                        ]
                    row += width_b

    def ladder(at):
        row = 0
        for first, count, half in pieces:
            low = halves.index(half) * span
            weights = amp_buf[at, :, low : low + span, :].reshape(step_d * span, amp_buf.shape[3])
            size = count * width_b
            out_ref[first * width_b : first * width_b + size, :] += jnp.dot(
                integral_ref[at, row : row + size, :], weights, preferred_element_type=jnp.float32
            )
            row += size

    @pl.when(step == 0)
    def _():
        for m in range(ranks):
            right_copy(0, 0, 0, m).start()
        for k, (_, count, _) in enumerate(pieces):
            for a in range(0, count, 4):
                left_copy(k, a).start()
        out_ref[...] = total_ref[...]

    amp_copy(step, slot).start()
    if steps > 1:

        @pl.when(step + 1 < steps)
        def _():
            fetch_right(step + 1, 1 - slot)

    for m in range(ranks):
        right_copy(0, 0, slot, m).wait()

    @pl.when(step == 0)
    def _():
        integrals(0, True)

    if steps > 1:

        @pl.when(step > 0)
        def _():
            amp_copy(0, 1 - slot).wait()
            ladder(1 - slot)
            integrals(slot, False)

    @pl.when(step == steps - 1)
    def _():
        amp_copy(0, slot).wait()
        ladder(slot)


def add_ladder(place, total, amp, first_d, span, lefts, rights, pieces, step_d):
    _, width_b, depth = rights[0][0].shape
    ranks = len(rights[0])
    pair_count = amp.shape[2]
    chunk_steps = tuple(blocks[0].shape[0] // step_d for blocks in rights)
    steps = sum(chunk_steps)
    halves = {half for _, _, half in pieces}
    count_a = sum(count for _, count, _ in pieces)
    columns = count_a * span
    flops = 2 * steps * step_d * width_b * columns * (depth * ranks + pair_count)
    blocks = [block for chunk in rights for block in chunk]
    anywhere = pl.BlockSpec(memory_space=pl.ANY)
    return pl.pallas_call(
        functools.partial(
            ladder_kernel,
            pieces=pieces,
            chunk_steps=chunk_steps,
            ranks=ranks,
            first_step=first_d // step_d,
            span=span,
        ),
        out_shape=jax.ShapeDtypeStruct(total.shape, total.dtype),
        grid_spec=pltpu.PrefetchScalarGridSpec(
            num_scalar_prefetch=1,
            grid=(steps,),
            in_specs=[pl.BlockSpec(total.shape, lambda s, _: (0, 0))]
            + [anywhere] * (1 + len(lefts) + len(blocks)),
            out_specs=pl.BlockSpec(total.shape, lambda s, _: (0, 0)),
            scratch_shapes=[pltpu.VMEM(x.shape, x.dtype) for x in lefts]
            + [
                pltpu.VMEM((2, ranks, step_d, width_b, depth), jnp.bfloat16),
                pltpu.VMEM((2, step_d, span * len(halves), pair_count), jnp.bfloat16),
                pltpu.VMEM((2, count_a * width_b, step_d * span), jnp.bfloat16),
                pltpu.SemaphoreType.DMA((len(lefts), -(-max(n for _, n, _ in pieces) // 4))),
                pltpu.SemaphoreType.DMA((2, ranks)),
                pltpu.SemaphoreType.DMA((2,)),
            ],
        ),
        input_output_aliases={1: 0},
        compiler_params=pltpu.CompilerParams(vmem_limit_bytes=VMEM_BYTES),
        cost_estimate=pl.CostEstimate(
            flops=flops // 20,
            bytes_accessed=2 * depth * ranks * (columns + steps * step_d * width_b),
            transcendentals=0,
        ),
    )(place, total, amp, *lefts, *blocks)


VMEM_BYTES = 62 * 2**20
SMALL_COST = pl.CostEstimate(flops=0, bytes_accessed=2**16, transcendentals=0)


def turn_kernel(in_ref, out_ref, wide_ref):
    outer, inner, width = in_ref.shape
    for k in range(width // 128):
        lanes = slice(k * 128, (k + 1) * 128)
        wide_ref[k] = in_ref[:, :, lanes].astype(jnp.float32).reshape(outer * inner, 128)
        for i in range(inner):
            out_ref[i, :, lanes] = wide_ref[k, pl.ds(i, outer, stride=inner), :].astype(out_ref.dtype)


def turn(array, start, size):
    outer, _, width = array.shape
    inner = 16
    if start % inner or size % inner or width % 128 or outer % 16:
        return jnp.transpose(array[:, start : start + size], (1, 0, 2))
    block = math.gcd(outer, 64)
    return pl.pallas_call(
        turn_kernel,
        out_shape=jax.ShapeDtypeStruct((size, outer, width), array.dtype),
        grid=(size // inner, outer // block),
        in_specs=[pl.BlockSpec((block, inner, width), lambda i, j: (j, start // inner + i, 0))],
        out_specs=pl.BlockSpec((inner, block, width), lambda i, j: (i, j, 0)),
        scratch_shapes=[pltpu.VMEM((width // 128, block * inner, 128), jnp.float32)],
        compiler_params=pltpu.CompilerParams(vmem_limit_bytes=VMEM_BYTES),
        cost_estimate=SMALL_COST,
    )(array)


def split_kernel(in_ref, *refs, pieces, span):
    wide_ref = refs[-1]
    rows, count_a, _ = in_ref.shape
    for half in sorted({half for _, _, half in pieces}):
        lanes = slice(half * span, (half + 1) * span)
        wide_ref[half] = in_ref[:, :, lanes].astype(jnp.float32).reshape(rows * count_a, span)
    for (first, count, half), out_ref in zip(pieces, refs):
        for a in range(count):
            picked = wide_ref[half, pl.ds(first + a, rows, stride=count_a), :]
            out_ref[:, a * span : (a + 1) * span] = picked.astype(out_ref.dtype)


def split_left(array, pieces, span):
    rows, count_a, span_c = array.shape
    block = math.gcd(rows, 256)
    return pl.pallas_call(
        functools.partial(split_kernel, pieces=pieces, span=span),
        out_shape=[jax.ShapeDtypeStruct((rows, count * span), array.dtype) for _, count, _ in pieces],
        grid=(rows // block,),
        in_specs=[pl.BlockSpec((block, count_a, span_c), lambda i: (i, 0, 0))],
        out_specs=[pl.BlockSpec((block, count * span), lambda i: (i, 0)) for _, count, _ in pieces],
        scratch_shapes=[pltpu.VMEM((span_c // span, block * count_a, span), jnp.float32)],
        compiler_params=pltpu.CompilerParams(vmem_limit_bytes=VMEM_BYTES),
        cost_estimate=SMALL_COST,
    )(array)


def swap(block, axis, bit, size):
    return lax.ppermute(block, axis, [(i, i ^ bit) for i in range(size)])


def on_device(left_factor, right_factor, amplitudes, *, row_size, col_size):
    width_a = left_factor.shape[1]
    span_c = left_factor.shape[2]
    width_b, span_d, depth = right_factor.shape
    pair_count = amplitudes.shape[2]
    span = span_c // 2
    place = lax.axis_index("row").astype(jnp.int32).reshape(1)

    pieces = [(f * width_a // 8, n * width_a // 8, h) for f, n, h in PIECES]

    chunks = [share * span_d // 16 for share in CHUNK_SHARES]
    starts = [sum(chunks[:j]) for j in range(len(chunks))]
    step_d = math.gcd(16, *chunks)

    together = lax.optimization_barrier
    far_bit = row_size // 2
    near_bits = [1 << k for k in reversed(range(row_size.bit_length() - 2))]

    def spread(held):
        for bit in near_bits:
            held = held | {m ^ bit: swap(x, "row", bit, row_size) for m, x in held.items()}
        return held

    parts = split_left(left_factor, pieces, span)
    parts, right_factor = together((parts, right_factor))
    owns = [turn(right_factor, starts[0], chunks[0])]
    owns[0], right_factor = together((owns[0], right_factor))

    lefts = [lax.all_gather(part, "col", axis=0, tiled=True) for part in parts]

    total = jnp.zeros((width_a * width_b, pair_count), jnp.float32)
    rights = [spread({0: owns[0]})]
    for j, calls in enumerate(STAGES):
        moving = j < len(chunks)
        if moving:
            far = swap(owns[j], "row", far_bit, row_size)
        if j == 0:
            owns.append(turn(right_factor, starts[1], chunks[1]))
        if j == 1:
            owns += [turn(right_factor, s, n) for s, n in zip(starts[2:], chunks[2:])]
            owns, amplitudes = together((owns, amplitudes))
            amp = jnp.transpose(amplitudes, (1, 0, 2))
        for chosen, js in calls:
            total = add_ladder(
                place, total, amp, starts[js[0]], span,
                [lefts[k] for k in chosen],
                [[rights[i][m] for m in range(row_size)] for i in js],
                [pieces[k] for k in chosen], step_d,
            )
        if moving:
            if j == 0:
                far, total, owns, right_factor, amplitudes = together(
                    (far, total, owns, right_factor, amplitudes)
                )
            elif j == 1:
                far, total, owns, amp, rights = together((far, total, owns, amp, rights))
            else:
                far, total, owns = together((far, total, owns))
            rights[j] |= spread({far_bit: far})
            if j + 1 < len(chunks):
                rights.append(spread({0: owns[j + 1]}))
    owners = row_size * col_size
    shares = total.T.reshape(owners, pair_count // owners, width_a * width_b)
    return lax.all_to_all(shares, ("row", "col"), 0, 0, tiled=True).sum(axis=0)


STAGES = (
    (),
    (),
    (((0,), (0, 1)),),
    (((1,), (0, 1)), ((0,), (2,))),
    (((1,), (2,)), ((0, 1), (3,)), ((2,), (0,))),
    (((2,), (1, 2, 3)), ((1, 2), (4,))),
    (((0,), (4,)), ((0, 1, 2), (5,))),
)


def solution(mesh):
    return jax.shard_map(
        functools.partial(on_device, row_size=mesh.shape["row"], col_size=mesh.shape["col"]),
        mesh=mesh,
        in_specs=(
            P(("parts", "col"), None, "row"),
            P("parts", "col", "row"),
            P("row", "col", "parts"),
        ),
        out_specs=P(("parts", "row", "col"), None),
        check_vma=False,
    )
```

```python
import functools
import math

import jax
import jax.numpy as jnp
from jax import lax
from jax.experimental import pallas as pl
from jax.experimental.pallas import tpu as pltpu
from jax.sharding import PartitionSpec as P

CHUNK_SHARES = (2, 3, 3, 2, 2, 2, 2)
PIECES = ((0, 8, 0), (0, 4, 1), (4, 4, 1))


def ladder_kernel(place_ref, total_ref, amp_ref, *refs, pieces, chunk_steps, ranks, first_step, span):
    count_l, count_r = len(pieces), len(chunk_steps) * ranks
    left_refs, right_refs = refs[:count_l], refs[count_l : count_l + count_r]
    out_ref = refs[count_l + count_r]
    rest = refs[count_l + count_r + 1 :]
    left_bufs = rest[:count_l]
    right_buf, amp_buf, integral_ref, left_sem, right_sem, amp_sem, total_sem = rest[count_l:]
    _, _, step_d, width_b, depth = right_buf.shape
    steps = sum(chunk_steps)
    halves = sorted({half for _, _, half in pieces})
    low_c, wide_c = halves[0] * span, len(halves) * span
    step = pl.program_id(0)
    slot = lax.rem(step, 2)
    place = place_ref[0]

    def left_copies(k, a):
        columns = pl.ds(a * span, min(pieces[k][1], 4) * span)
        return [
            pltpu.make_async_copy(
                left_refs[k].at[pl.ds(m * depth, depth), columns],
                left_bufs[k].at[pl.ds(m * depth, depth), columns],
                left_sem.at[k, a // 4, m],
            )
            for m in range(ranks)
        ]

    def total_copy():
        return pltpu.make_async_copy(total_ref, out_ref, total_sem)

    def right_copy(j, offset, to, m):
        source = right_refs[j * ranks + m].at[pl.ds(offset * step_d, step_d)]
        return pltpu.make_async_copy(source, right_buf.at[to, m], right_sem.at[to, m])

    def amp_copy(at, to):
        rows = pl.ds((first_step + at) * step_d, step_d)
        return pltpu.make_async_copy(
            amp_ref.at[rows, pl.ds(low_c, wide_c)], amp_buf.at[to], amp_sem.at[to]
        )

    def fetch_right(at, to):
        begin = 0
        for j, n in enumerate(chunk_steps):

            @pl.when((at >= begin) & (at < begin + n))
            def _():
                for m in range(ranks):
                    right_copy(j, at - begin, to, m).start()

            begin += n

    def integrals(to, first):
        row = 0
        for k, (_, count, _) in enumerate(pieces):
            wide = min(count, 4)
            for a in range(0, count, wide):
                if first:
                    for copy in left_copies(k, a):
                        copy.wait()
                product = None
                for m in range(ranks):
                    start = pl.multiple_of((place ^ m) * depth, depth)
                    term = jnp.dot(
                        right_buf[to, m].reshape(step_d * width_b, depth),
                        left_bufs[k][pl.ds(start, depth), a * span : (a + wide) * span],
                        preferred_element_type=jnp.float32,
                    )
                    product = term if product is None else product + term
                rounded = product.astype(jnp.bfloat16)
                for i in range(wide):
                    for d in range(step_d):
                        integral_ref[to, row : row + width_b, d * span : (d + 1) * span] = rounded[
                            d * width_b : (d + 1) * width_b, i * span : (i + 1) * span
                        ]
                    row += width_b

    def ladder(at):
        row = 0
        for first, count, half in pieces:
            low = halves.index(half) * span
            weights = amp_buf[at, :, low : low + span, :].reshape(step_d * span, amp_buf.shape[3])
            size = count * width_b
            out_ref[first * width_b : first * width_b + size, :] += jnp.dot(
                integral_ref[at, row : row + size, :], weights, preferred_element_type=jnp.float32
            )
            row += size

    @pl.when(step == 0)
    def _():
        for m in range(ranks):
            right_copy(0, 0, 0, m).start()
        for k, (_, count, _) in enumerate(pieces):
            for a in range(0, count, 4):
                for copy in left_copies(k, a):
                    copy.start()
        total_copy().start()

    amp_copy(step, slot).start()
    if steps > 1:

        @pl.when(step + 1 < steps)
        def _():
            fetch_right(step + 1, 1 - slot)

    for m in range(ranks):
        right_copy(0, 0, slot, m).wait()

    @pl.when(step == 0)
    def _():
        integrals(0, True)
        total_copy().wait()

    if steps > 1:

        @pl.when(step > 0)
        def _():
            amp_copy(0, 1 - slot).wait()
            ladder(1 - slot)
            integrals(slot, False)

    @pl.when(step == steps - 1)
    def _():
        amp_copy(0, slot).wait()
        ladder(slot)


def add_ladder(place, total, amp, first_d, span, lefts, rights, pieces, step_d):
    _, width_b, depth = rights[0][0].shape
    ranks = len(rights[0])
    pair_count = amp.shape[2]
    chunk_steps = tuple(blocks[0].shape[0] // step_d for blocks in rights)
    steps = sum(chunk_steps)
    halves = {half for _, _, half in pieces}
    count_a = sum(count for _, count, _ in pieces)
    columns = count_a * span
    flops = 2 * steps * step_d * width_b * columns * (depth * ranks + pair_count)
    blocks = [block for chunk in rights for block in chunk]
    anywhere = pl.BlockSpec(memory_space=pl.ANY)
    return pl.pallas_call(
        functools.partial(
            ladder_kernel,
            pieces=pieces,
            chunk_steps=chunk_steps,
            ranks=ranks,
            first_step=first_d // step_d,
            span=span,
        ),
        out_shape=jax.ShapeDtypeStruct(total.shape, total.dtype),
        grid_spec=pltpu.PrefetchScalarGridSpec(
            num_scalar_prefetch=1,
            grid=(steps,),
            in_specs=[anywhere] * (2 + len(lefts) + len(blocks)),
            out_specs=pl.BlockSpec(total.shape, lambda s, _: (0, 0)),
            scratch_shapes=[pltpu.VMEM(x.shape, x.dtype) for x in lefts]
            + [
                pltpu.VMEM((2, ranks, step_d, width_b, depth), jnp.bfloat16),
                pltpu.VMEM((2, step_d, span * len(halves), pair_count), jnp.bfloat16),
                pltpu.VMEM((2, count_a * width_b, step_d * span), jnp.bfloat16),
                pltpu.SemaphoreType.DMA((len(lefts), -(-max(n for _, n, _ in pieces) // 4), ranks)),
                pltpu.SemaphoreType.DMA((2, ranks)),
                pltpu.SemaphoreType.DMA((2,)),
                pltpu.SemaphoreType.DMA(()),
            ],
        ),
        input_output_aliases={1: 0},
        compiler_params=pltpu.CompilerParams(vmem_limit_bytes=VMEM_BYTES),
        cost_estimate=pl.CostEstimate(
            flops=flops // 20,
            bytes_accessed=2 * depth * ranks * (columns + steps * step_d * width_b),
            transcendentals=0,
        ),
    )(place, total, amp, *lefts, *blocks)


VMEM_BYTES = 62 * 2**20
SMALL_COST = pl.CostEstimate(flops=0, bytes_accessed=2**16, transcendentals=0)


def turn_kernel(in_ref, out_ref, wide_ref):
    outer, inner, width = in_ref.shape
    for k in range(width // 128):
        lanes = slice(k * 128, (k + 1) * 128)
        wide_ref[k] = in_ref[:, :, lanes].astype(jnp.float32).reshape(outer * inner, 128)
        for i in range(inner):
            out_ref[i, :, lanes] = wide_ref[k, pl.ds(i, outer, stride=inner), :].astype(out_ref.dtype)


def turn(array, start, size):
    outer, _, width = array.shape
    inner = 16
    if start % inner or size % inner or width % 128 or outer % 16:
        return jnp.transpose(array[:, start : start + size], (1, 0, 2))
    block = math.gcd(outer, 64)
    return pl.pallas_call(
        turn_kernel,
        out_shape=jax.ShapeDtypeStruct((size, outer, width), array.dtype),
        grid=(size // inner, outer // block),
        in_specs=[pl.BlockSpec((block, inner, width), lambda i, j: (j, start // inner + i, 0))],
        out_specs=pl.BlockSpec((inner, block, width), lambda i, j: (i, j, 0)),
        scratch_shapes=[pltpu.VMEM((width // 128, block * inner, 128), jnp.float32)],
        compiler_params=pltpu.CompilerParams(vmem_limit_bytes=VMEM_BYTES),
        cost_estimate=SMALL_COST,
    )(array)


def split_kernel(in_ref, *refs, pieces, span):
    wide_ref = refs[-1]
    rows, count_a, _ = in_ref.shape
    for half in sorted({half for _, _, half in pieces}):
        lanes = slice(half * span, (half + 1) * span)
        wide_ref[half] = in_ref[:, :, lanes].astype(jnp.float32).reshape(rows * count_a, span)
    for (first, count, half), out_ref in zip(pieces, refs):
        for a in range(count):
            picked = wide_ref[half, pl.ds(first + a, rows, stride=count_a), :]
            out_ref[:, a * span : (a + 1) * span] = picked.astype(out_ref.dtype)


def split_left(array, pieces, span):
    rows, count_a, span_c = array.shape
    block = math.gcd(rows, 256)
    return pl.pallas_call(
        functools.partial(split_kernel, pieces=pieces, span=span),
        out_shape=[jax.ShapeDtypeStruct((rows, count * span), array.dtype) for _, count, _ in pieces],
        grid=(rows // block,),
        in_specs=[pl.BlockSpec((block, count_a, span_c), lambda i: (i, 0, 0))],
        out_specs=[pl.BlockSpec((block, count * span), lambda i: (i, 0)) for _, count, _ in pieces],
        scratch_shapes=[pltpu.VMEM((span_c // span, block * count_a, span), jnp.float32)],
        compiler_params=pltpu.CompilerParams(vmem_limit_bytes=VMEM_BYTES),
        cost_estimate=SMALL_COST,
    )(array)


def swap(block, axis, bit, size):
    return lax.ppermute(block, axis, [(i, i ^ bit) for i in range(size)])


def on_device(left_factor, right_factor, amplitudes, *, row_size, col_size):
    width_a = left_factor.shape[1]
    span_c = left_factor.shape[2]
    width_b, span_d, depth = right_factor.shape
    pair_count = amplitudes.shape[2]
    span = span_c // 2
    place = lax.axis_index("row").astype(jnp.int32).reshape(1)

    pieces = [(f * width_a // 8, n * width_a // 8, h) for f, n, h in PIECES]

    chunks = [share * span_d // 16 for share in CHUNK_SHARES]
    starts = [sum(chunks[:j]) for j in range(len(chunks))]
    step_d = math.gcd(16, *chunks)

    together = lax.optimization_barrier
    far_bit = row_size // 2
    near_bits = [1 << k for k in reversed(range(row_size.bit_length() - 2))]

    def spread(held):
        for bit in near_bits:
            held = held | {m ^ bit: swap(x, "row", bit, row_size) for m, x in held.items()}
        return held

    parts = split_left(left_factor, pieces, span)
    parts, right_factor = together((parts, right_factor))
    owns = [turn(right_factor, starts[0], chunks[0])]
    owns[0], right_factor = together((owns[0], right_factor))

    lefts = [lax.all_gather(part, "col", axis=0, tiled=True) for part in parts]

    total = jnp.zeros((width_a * width_b, pair_count), jnp.float32)
    rights = [spread({0: owns[0]})]
    for j, calls in enumerate(STAGES):
        moving = j < len(chunks)
        if moving:
            far = swap(owns[j], "row", far_bit, row_size)
        if j == 0:
            owns.append(turn(right_factor, starts[1], chunks[1]))
        if j == 1:
            owns += [turn(right_factor, s, n) for s, n in zip(starts[2:], chunks[2:])]
            owns, amplitudes = together((owns, amplitudes))
            amp = jnp.transpose(amplitudes, (1, 0, 2))
        for chosen, js in calls:
            total = add_ladder(
                place, total, amp, starts[js[0]], span,
                [lefts[k] for k in chosen],
                [[rights[i][m] for m in range(row_size)] for i in js],
                [pieces[k] for k in chosen], step_d,
            )
        if moving:
            if j == 0:
                far, total, owns, right_factor, amplitudes = together(
                    (far, total, owns, right_factor, amplitudes)
                )
            elif j == 1:
                far, total, owns, amp, rights = together((far, total, owns, amp, rights))
            else:
                far, total, owns = together((far, total, owns))
            rights[j] |= spread({far_bit: far})
            if j + 1 < len(chunks):
                rights.append(spread({0: owns[j + 1]}))
    owners = row_size * col_size
    shares = total.T.reshape(owners, pair_count // owners, width_a * width_b)
    return lax.all_to_all(shares, ("row", "col"), 0, 0, tiled=True).sum(axis=0)


STAGES = (
    (),
    (),
    (((0,), (0, 1)),),
    (((0,), (2,)),),
    (((1,), (0, 1, 2)), ((0, 1), (3,))),
    (((0, 1), (4,)), ((2,), (0, 1))),
    (((2,), (2, 3)), ((0, 1, 2), (5,))),
    (((2,), (4,)), ((0, 1, 2), (6,))),
)


def solution(mesh):
    return jax.shard_map(
        functools.partial(on_device, row_size=mesh.shape["row"], col_size=mesh.shape["col"]),
        mesh=mesh,
        in_specs=(
            P(("parts", "col"), None, "row"),
            P("parts", "col", "row"),
            P("row", "col", "parts"),
        ),
        out_specs=P(("parts", "row", "col"), None),
        check_vma=False,
    )
```

```python
import functools
import math

import jax
import jax.numpy as jnp
from jax import lax
from jax.experimental import pallas as pl
from jax.experimental.pallas import tpu as pltpu
from jax.sharding import PartitionSpec as P

CHUNK_SHARES = (2, 3, 3, 2, 2, 2, 2)
PIECES = ((0, 8, 0), (0, 4, 1), (4, 4, 1))


def ladder_kernel(place_ref, total_ref, amp_ref, *refs, pieces, chunk_steps, ranks, first_step, span):
    count_l, count_r = len(pieces), len(chunk_steps) * ranks
    left_refs, right_refs = refs[:count_l], refs[count_l : count_l + count_r]
    out_ref = refs[count_l + count_r]
    rest = refs[count_l + count_r + 1 :]
    left_bufs = rest[:count_l]
    right_buf, amp_buf, integral_ref, left_sem, right_sem, amp_sem, total_sem = rest[count_l:]
    _, _, step_d, width_b, depth = right_buf.shape
    steps = sum(chunk_steps)
    halves = sorted({half for _, _, half in pieces})
    low_c, wide_c = halves[0] * span, len(halves) * span
    step = pl.program_id(0)
    slot = lax.rem(step, 2)
    place = place_ref[0]

    def left_copies(k, a):
        columns = pl.ds(a * span, min(pieces[k][1], 4) * span)
        return [
            pltpu.make_async_copy(
                left_refs[k].at[pl.ds(m * depth, depth), columns],
                left_bufs[k].at[pl.ds(m * depth, depth), columns],
                left_sem.at[k, a // 4, m],
            )
            for m in range(ranks)
        ]

    def total_copy():
        return pltpu.make_async_copy(total_ref, out_ref, total_sem)

    def right_copy(j, offset, to, m):
        source = right_refs[j * ranks + m].at[pl.ds(offset * step_d, step_d)]
        return pltpu.make_async_copy(source, right_buf.at[to, m], right_sem.at[to, m])

    def amp_copy(at, to):
        rows = pl.ds((first_step + at) * step_d, step_d)
        return pltpu.make_async_copy(
            amp_ref.at[rows, pl.ds(low_c, wide_c)], amp_buf.at[to], amp_sem.at[to]
        )

    def fetch_right(at, to):
        begin = 0
        for j, n in enumerate(chunk_steps):

            @pl.when((at >= begin) & (at < begin + n))
            def _():
                for m in range(ranks):
                    right_copy(j, at - begin, to, m).start()

            begin += n

    def integrals(to, first):
        row = 0
        for k, (_, count, _) in enumerate(pieces):
            wide = min(count, 4)
            for a in range(0, count, wide):
                if first:
                    for copy in left_copies(k, a):
                        copy.wait()
                product = None
                for m in range(ranks):
                    start = pl.multiple_of((place ^ m) * depth, depth)
                    term = jnp.dot(
                        right_buf[to, m].reshape(step_d * width_b, depth),
                        left_bufs[k][pl.ds(start, depth), a * span : (a + wide) * span],
                        preferred_element_type=jnp.float32,
                    )
                    product = term if product is None else product + term
                rounded = product.astype(jnp.bfloat16)
                for i in range(wide):
                    for d in range(step_d):
                        integral_ref[to, row : row + width_b, d * span : (d + 1) * span] = rounded[
                            d * width_b : (d + 1) * width_b, i * span : (i + 1) * span
                        ]
                    row += width_b

    def ladder(at):
        row = 0
        for first, count, half in pieces:
            low = halves.index(half) * span
            weights = amp_buf[at, :, low : low + span, :].reshape(step_d * span, amp_buf.shape[3])
            size = count * width_b
            out_ref[first * width_b : first * width_b + size, :] += jnp.dot(
                integral_ref[at, row : row + size, :], weights, preferred_element_type=jnp.float32
            )
            row += size

    @pl.when(step == 0)
    def _():
        for m in range(ranks):
            right_copy(0, 0, 0, m).start()
        for k, (_, count, _) in enumerate(pieces):
            for a in range(0, count, 4):
                for copy in left_copies(k, a):
                    copy.start()
        total_copy().start()

    amp_copy(step, slot).start()
    if steps > 1:

        @pl.when(step + 1 < steps)
        def _():
            fetch_right(step + 1, 1 - slot)

    for m in range(ranks):
        right_copy(0, 0, slot, m).wait()

    @pl.when(step == 0)
    def _():
        integrals(0, True)
        total_copy().wait()

    if steps > 1:

        @pl.when(step > 0)
        def _():
            amp_copy(0, 1 - slot).wait()
            ladder(1 - slot)
            integrals(slot, False)

    @pl.when(step == steps - 1)
    def _():
        amp_copy(0, slot).wait()
        ladder(slot)


def add_ladder(place, total, amp, first_d, span, lefts, rights, pieces, step_d):
    _, width_b, depth = rights[0][0].shape
    ranks = len(rights[0])
    pair_count = amp.shape[2]
    chunk_steps = tuple(blocks[0].shape[0] // step_d for blocks in rights)
    steps = sum(chunk_steps)
    halves = {half for _, _, half in pieces}
    count_a = sum(count for _, count, _ in pieces)
    columns = count_a * span
    flops = 2 * steps * step_d * width_b * columns * (depth * ranks + pair_count)
    blocks = [block for chunk in rights for block in chunk]
    anywhere = pl.BlockSpec(memory_space=pl.ANY)
    return pl.pallas_call(
        functools.partial(
            ladder_kernel,
            pieces=pieces,
            chunk_steps=chunk_steps,
            ranks=ranks,
            first_step=first_d // step_d,
            span=span,
        ),
        out_shape=jax.ShapeDtypeStruct(total.shape, total.dtype),
        grid_spec=pltpu.PrefetchScalarGridSpec(
            num_scalar_prefetch=1,
            grid=(steps,),
            in_specs=[anywhere] * (2 + len(lefts) + len(blocks)),
            out_specs=pl.BlockSpec(total.shape, lambda s, _: (0, 0)),
            scratch_shapes=[pltpu.VMEM(x.shape, x.dtype) for x in lefts]
            + [
                pltpu.VMEM((2, ranks, step_d, width_b, depth), jnp.bfloat16),
                pltpu.VMEM((2, step_d, span * len(halves), pair_count), jnp.bfloat16),
                pltpu.VMEM((2, count_a * width_b, step_d * span), jnp.bfloat16),
                pltpu.SemaphoreType.DMA((len(lefts), -(-max(n for _, n, _ in pieces) // 4), ranks)),
                pltpu.SemaphoreType.DMA((2, ranks)),
                pltpu.SemaphoreType.DMA((2,)),
                pltpu.SemaphoreType.DMA(()),
            ],
        ),
        input_output_aliases={1: 0},
        compiler_params=pltpu.CompilerParams(vmem_limit_bytes=VMEM_BYTES),
        cost_estimate=pl.CostEstimate(
            flops=flops // 20,
            bytes_accessed=2 * depth * ranks * (columns + steps * step_d * width_b),
            transcendentals=0,
        ),
    )(place, total, amp, *lefts, *blocks)


VMEM_BYTES = 62 * 2**20
SMALL_COST = pl.CostEstimate(flops=0, bytes_accessed=2**16, transcendentals=0)


def turn_kernel(in_ref, out_ref, wide_ref):
    outer, inner, width = in_ref.shape
    for k in range(width // 128):
        lanes = slice(k * 128, (k + 1) * 128)
        wide_ref[k] = in_ref[:, :, lanes].astype(jnp.float32).reshape(outer * inner, 128)
        for i in range(inner):
            out_ref[i, :, lanes] = wide_ref[k, pl.ds(i, outer, stride=inner), :].astype(out_ref.dtype)


def turn(array, start, size):
    outer, _, width = array.shape
    inner = 16
    if start % inner or size % inner or width % 128 or outer % 16:
        return jnp.transpose(array[:, start : start + size], (1, 0, 2))
    block = math.gcd(outer, 64)
    return pl.pallas_call(
        turn_kernel,
        out_shape=jax.ShapeDtypeStruct((size, outer, width), array.dtype),
        grid=(size // inner, outer // block),
        in_specs=[pl.BlockSpec((block, inner, width), lambda i, j: (j, start // inner + i, 0))],
        out_specs=pl.BlockSpec((inner, block, width), lambda i, j: (i, j, 0)),
        scratch_shapes=[pltpu.VMEM((width // 128, block * inner, 128), jnp.float32)],
        compiler_params=pltpu.CompilerParams(vmem_limit_bytes=VMEM_BYTES),
        cost_estimate=SMALL_COST,
    )(array)


def split_kernel(in_ref, *refs, pieces, span):
    wide_ref = refs[-1]
    rows, count_a, _ = in_ref.shape
    wide_ref[...] = in_ref[...].astype(jnp.float32).reshape(rows * count_a, span)
    for (first, count, _), out_ref in zip(pieces, refs):
        for a in range(count):
            picked = wide_ref[pl.ds(first + a, rows, stride=count_a), :]
            out_ref[:, a * span : (a + 1) * span] = picked.astype(out_ref.dtype)


def split_left(array, pieces, span):
    rows, count_a, _ = array.shape
    half = pieces[0][2]
    block = math.gcd(rows, 256)
    return pl.pallas_call(
        functools.partial(split_kernel, pieces=pieces, span=span),
        out_shape=[jax.ShapeDtypeStruct((rows, count * span), array.dtype) for _, count, _ in pieces],
        grid=(rows // block,),
        in_specs=[pl.BlockSpec((block, count_a, span), lambda i: (i, 0, half))],
        out_specs=[pl.BlockSpec((block, count * span), lambda i: (i, 0)) for _, count, _ in pieces],
        scratch_shapes=[pltpu.VMEM((block * count_a, span), jnp.float32)],
        compiler_params=pltpu.CompilerParams(vmem_limit_bytes=VMEM_BYTES),
        cost_estimate=SMALL_COST,
    )(array)


def swap(block, axis, bit, size):
    return lax.ppermute(block, axis, [(i, i ^ bit) for i in range(size)])


def on_device(left_factor, right_factor, amplitudes, *, row_size, col_size):
    width_a = left_factor.shape[1]
    span_c = left_factor.shape[2]
    width_b, span_d, depth = right_factor.shape
    pair_count = amplitudes.shape[2]
    span = span_c // 2
    place = lax.axis_index("row").astype(jnp.int32).reshape(1)

    pieces = [(f * width_a // 8, n * width_a // 8, h) for f, n, h in PIECES]

    chunks = [share * span_d // 16 for share in CHUNK_SHARES]
    starts = [sum(chunks[:j]) for j in range(len(chunks))]
    step_d = math.gcd(16, *chunks)

    together = lax.optimization_barrier
    far_bit = row_size // 2
    near_bits = [1 << k for k in reversed(range(row_size.bit_length() - 2))]

    def spread(held):
        for bit in near_bits:
            held = held | {m ^ bit: swap(x, "row", bit, row_size) for m, x in held.items()}
        return held

    parts = split_left(left_factor, pieces[:1], span)
    parts, right_factor, left_factor = together((parts, right_factor, left_factor))
    owns = [turn(right_factor, starts[0], chunks[0])]
    owns[0], right_factor, left_factor = together((owns[0], right_factor, left_factor))

    def gathered(parts):
        return [lax.all_gather(part, "col", axis=0, tiled=True) for part in parts]

    lefts = gathered(parts)
    total = jnp.zeros((width_a * width_b, pair_count), jnp.float32)
    rights = [spread({0: owns[0]})]
    for j, calls in enumerate(STAGES):
        moving = j < len(chunks)
        if moving:
            far = swap(owns[j], "row", far_bit, row_size)
        if j == 0:
            owns.append(turn(right_factor, starts[1], chunks[1]))
        if j == 1:
            parts = split_left(left_factor, pieces[1:], span)
            lefts += gathered(parts)
            parts, right_factor = together((parts, right_factor))
            owns += [turn(right_factor, s, n) for s, n in zip(starts[2:], chunks[2:])]
            owns, amplitudes = together((owns, amplitudes))
            amp = jnp.transpose(amplitudes, (1, 0, 2))
        for chosen, js in calls:
            total = add_ladder(
                place, total, amp, starts[js[0]], span,
                [lefts[k] for k in chosen],
                [[rights[i][m] for m in range(row_size)] for i in js],
                [pieces[k] for k in chosen], step_d,
            )
        if moving:
            if j == 0:
                far, total, right_factor, left_factor, amplitudes = together(
                    (far, total, right_factor, left_factor, amplitudes)
                )
            elif j == 1:
                far, total, amp, rights = together((far, total, amp, rights))
            else:
                far, total, owns = together((far, total, owns))
            rights[j] |= spread({far_bit: far})
            if j + 1 < len(chunks):
                rights.append(spread({0: owns[j + 1]}))
    owners = row_size * col_size
    shares = total.T.reshape(owners, pair_count // owners, width_a * width_b)
    return lax.all_to_all(shares, ("row", "col"), 0, 0, tiled=True).sum(axis=0)


STAGES = (
    (),
    (),
    (((0,), (0, 1)),),
    (((0,), (2,)),),
    (((1,), (0, 1, 2)), ((0, 1), (3,))),
    (((0, 1), (4,)), ((2,), (0, 1))),
    (((2,), (2, 3)), ((0, 1, 2), (5,))),
    (((2,), (4,)), ((0, 1, 2), (6,))),
)


def solution(mesh):
    return jax.shard_map(
        functools.partial(on_device, row_size=mesh.shape["row"], col_size=mesh.shape["col"]),
        mesh=mesh,
        in_specs=(
            P(("parts", "col"), None, "row"),
            P("parts", "col", "row"),
            P("row", "col", "parts"),
        ),
        out_specs=P(("parts", "row", "col"), None),
        check_vma=False,
    )
```

```python
import functools
import math

import jax
import jax.numpy as jnp
from jax import lax
from jax.experimental import pallas as pl
from jax.experimental.pallas import tpu as pltpu
from jax.sharding import PartitionSpec as P

CHUNK_SHARES = (2, 3, 3, 2, 2, 2, 2)
PIECES = ((0, 8, 0), (0, 4, 1), (4, 4, 1))


def ladder_kernel(place_ref, total_ref, amp_ref, *refs, pieces, chunk_steps, ranks, first_step, span):
    count_l, count_r = len(pieces), len(chunk_steps) * ranks
    left_refs, right_refs = refs[:count_l], refs[count_l : count_l + count_r]
    out_ref = refs[count_l + count_r]
    rest = refs[count_l + count_r + 1 :]
    left_bufs = rest[:count_l]
    right_buf, amp_buf, integral_ref, left_sem, right_sem, amp_sem, total_sem = rest[count_l:]
    _, _, step_d, width_b, depth = right_buf.shape
    steps = sum(chunk_steps)
    halves = sorted({half for _, _, half in pieces})
    low_c, wide_c = halves[0] * span, len(halves) * span
    step = pl.program_id(0)
    slot = lax.rem(step, 2)
    place = place_ref[0]

    def left_copies(k, a):
        columns = pl.ds(a * span, min(pieces[k][1], 4) * span)
        return [
            pltpu.make_async_copy(
                left_refs[k].at[pl.ds(m * depth, depth), columns],
                left_bufs[k].at[pl.ds(m * depth, depth), columns],
                left_sem.at[k, a // 4, m],
            )
            for m in range(ranks)
        ]

    def total_copy():
        return pltpu.make_async_copy(total_ref, out_ref, total_sem)

    def right_copy(j, offset, to, m):
        source = right_refs[j * ranks + m].at[pl.ds(offset * step_d, step_d)]
        return pltpu.make_async_copy(source, right_buf.at[to, m], right_sem.at[to, m])

    def amp_copy(at, to):
        rows = pl.ds((first_step + at) * step_d, step_d)
        return pltpu.make_async_copy(
            amp_ref.at[rows, pl.ds(low_c, wide_c)], amp_buf.at[to], amp_sem.at[to]
        )

    def fetch_right(at, to):
        begin = 0
        for j, n in enumerate(chunk_steps):

            @pl.when((at >= begin) & (at < begin + n))
            def _():
                for m in range(ranks):
                    right_copy(j, at - begin, to, m).start()

            begin += n

    def fetch_rest():
        total_copy().start()
        amp_copy(0, 0).start()
        if steps > 1:
            fetch_right(1, 1)

    def integrals(to, first):
        row = 0
        for k, (_, count, _) in enumerate(pieces):
            wide = min(count, 4)
            for a in range(0, count, wide):
                if first:
                    for copy in left_copies(k, a):
                        copy.wait()
                    if k == 0 and a == 0:
                        fetch_rest()
                product = None
                for m in range(ranks):
                    start = pl.multiple_of((place ^ m) * depth, depth)
                    term = jnp.dot(
                        right_buf[to, m].reshape(step_d * width_b, depth),
                        left_bufs[k][pl.ds(start, depth), a * span : (a + wide) * span],
                        preferred_element_type=jnp.float32,
                    )
                    product = term if product is None else product + term
                rounded = product.astype(jnp.bfloat16)
                for i in range(wide):
                    for d in range(step_d):
                        integral_ref[to, row : row + width_b, d * span : (d + 1) * span] = rounded[
                            d * width_b : (d + 1) * width_b, i * span : (i + 1) * span
                        ]
                    row += width_b

    def ladder(at):
        row = 0
        for first, count, half in pieces:
            low = halves.index(half) * span
            weights = amp_buf[at, :, low : low + span, :].reshape(step_d * span, amp_buf.shape[3])
            size = count * width_b
            out_ref[first * width_b : first * width_b + size, :] += jnp.dot(
                integral_ref[at, row : row + size, :], weights, preferred_element_type=jnp.float32
            )
            row += size

    @pl.when(step == 0)
    def _():
        for m in range(ranks):
            right_copy(0, 0, 0, m).start()
        for k, (_, count, _) in enumerate(pieces):
            for a in range(0, count, 4):
                for copy in left_copies(k, a):
                    copy.start()

    if steps > 1:

        @pl.when(step > 0)
        def _():
            amp_copy(step, slot).start()

        @pl.when((step > 0) & (step + 1 < steps))
        def _():
            fetch_right(step + 1, 1 - slot)

    for m in range(ranks):
        right_copy(0, 0, slot, m).wait()

    @pl.when(step == 0)
    def _():
        integrals(0, True)
        total_copy().wait()

    if steps > 1:

        @pl.when(step > 0)
        def _():
            amp_copy(0, 1 - slot).wait()
            ladder(1 - slot)
            integrals(slot, False)

    @pl.when(step == steps - 1)
    def _():
        amp_copy(0, slot).wait()
        ladder(slot)


def add_ladder(place, total, amp, first_d, span, lefts, rights, pieces, step_d):
    _, width_b, depth = rights[0][0].shape
    ranks = len(rights[0])
    pair_count = amp.shape[2]
    chunk_steps = tuple(blocks[0].shape[0] // step_d for blocks in rights)
    steps = sum(chunk_steps)
    halves = {half for _, _, half in pieces}
    count_a = sum(count for _, count, _ in pieces)
    columns = count_a * span
    flops = 2 * steps * step_d * width_b * columns * (depth * ranks + pair_count)
    blocks = [block for chunk in rights for block in chunk]
    anywhere = pl.BlockSpec(memory_space=pl.ANY)
    return pl.pallas_call(
        functools.partial(
            ladder_kernel,
            pieces=pieces,
            chunk_steps=chunk_steps,
            ranks=ranks,
            first_step=first_d // step_d,
            span=span,
        ),
        out_shape=jax.ShapeDtypeStruct(total.shape, total.dtype),
        grid_spec=pltpu.PrefetchScalarGridSpec(
            num_scalar_prefetch=1,
            grid=(steps,),
            in_specs=[anywhere] * (2 + len(lefts) + len(blocks)),
            out_specs=pl.BlockSpec(total.shape, lambda s, _: (0, 0)),
            scratch_shapes=[pltpu.VMEM(x.shape, x.dtype) for x in lefts]
            + [
                pltpu.VMEM((2, ranks, step_d, width_b, depth), jnp.bfloat16),
                pltpu.VMEM((2, step_d, span * len(halves), pair_count), jnp.bfloat16),
                pltpu.VMEM((2, count_a * width_b, step_d * span), jnp.bfloat16),
                pltpu.SemaphoreType.DMA((len(lefts), -(-max(n for _, n, _ in pieces) // 4), ranks)),
                pltpu.SemaphoreType.DMA((2, ranks)),
                pltpu.SemaphoreType.DMA((2,)),
                pltpu.SemaphoreType.DMA(()),
            ],
        ),
        input_output_aliases={1: 0},
        compiler_params=pltpu.CompilerParams(vmem_limit_bytes=VMEM_BYTES),
        cost_estimate=pl.CostEstimate(
            flops=flops // 20,
            bytes_accessed=2 * depth * ranks * (columns + steps * step_d * width_b),
            transcendentals=0,
        ),
    )(place, total, amp, *lefts, *blocks)


VMEM_BYTES = 62 * 2**20
SMALL_COST = pl.CostEstimate(flops=0, bytes_accessed=2**16, transcendentals=0)


def turn_kernel(in_ref, out_ref, wide_ref):
    outer, inner, width = in_ref.shape
    for k in range(width // 128):
        lanes = slice(k * 128, (k + 1) * 128)
        wide_ref[k] = in_ref[:, :, lanes].astype(jnp.float32).reshape(outer * inner, 128)
        for i in range(inner):
            out_ref[i, :, lanes] = wide_ref[k, pl.ds(i, outer, stride=inner), :].astype(out_ref.dtype)


def turn(array, start, size):
    outer, _, width = array.shape
    inner = 16
    if start % inner or size % inner or width % 128 or outer % 16:
        return jnp.transpose(array[:, start : start + size], (1, 0, 2))
    block = math.gcd(outer, 64)
    return pl.pallas_call(
        turn_kernel,
        out_shape=jax.ShapeDtypeStruct((size, outer, width), array.dtype),
        grid=(size // inner, outer // block),
        in_specs=[pl.BlockSpec((block, inner, width), lambda i, j: (j, start // inner + i, 0))],
        out_specs=pl.BlockSpec((inner, block, width), lambda i, j: (i, j, 0)),
        scratch_shapes=[pltpu.VMEM((width // 128, block * inner, 128), jnp.float32)],
        compiler_params=pltpu.CompilerParams(vmem_limit_bytes=VMEM_BYTES),
        cost_estimate=SMALL_COST,
    )(array)


def split_kernel(in_ref, *refs, pieces, span):
    wide_ref = refs[-1]
    rows, count_a, _ = in_ref.shape
    wide_ref[...] = in_ref[...].astype(jnp.float32).reshape(rows * count_a, span)
    for (first, count, _), out_ref in zip(pieces, refs):
        for a in range(count):
            picked = wide_ref[pl.ds(first + a, rows, stride=count_a), :]
            out_ref[:, a * span : (a + 1) * span] = picked.astype(out_ref.dtype)


def split_left(array, pieces, span):
    rows, count_a, _ = array.shape
    half = pieces[0][2]
    block = math.gcd(rows, 256)
    return pl.pallas_call(
        functools.partial(split_kernel, pieces=pieces, span=span),
        out_shape=[jax.ShapeDtypeStruct((rows, count * span), array.dtype) for _, count, _ in pieces],
        grid=(rows // block,),
        in_specs=[pl.BlockSpec((block, count_a, span), lambda i: (i, 0, half))],
        out_specs=[pl.BlockSpec((block, count * span), lambda i: (i, 0)) for _, count, _ in pieces],
        scratch_shapes=[pltpu.VMEM((block * count_a, span), jnp.float32)],
        compiler_params=pltpu.CompilerParams(vmem_limit_bytes=VMEM_BYTES),
        cost_estimate=SMALL_COST,
    )(array)


def swap(block, axis, bit, size):
    return lax.ppermute(block, axis, [(i, i ^ bit) for i in range(size)])


def on_device(left_factor, right_factor, amplitudes, *, row_size, col_size):
    width_a = left_factor.shape[1]
    span_c = left_factor.shape[2]
    width_b, span_d, depth = right_factor.shape
    pair_count = amplitudes.shape[2]
    span = span_c // 2
    place = lax.axis_index("row").astype(jnp.int32).reshape(1)

    pieces = [(f * width_a // 8, n * width_a // 8, h) for f, n, h in PIECES]

    chunks = [share * span_d // 16 for share in CHUNK_SHARES]
    starts = [sum(chunks[:j]) for j in range(len(chunks))]
    step_d = math.gcd(16, *chunks)

    together = lax.optimization_barrier
    far_bit = row_size // 2
    near_bits = [1 << k for k in reversed(range(row_size.bit_length() - 2))]

    def spread(held):
        for bit in near_bits:
            held = held | {m ^ bit: swap(x, "row", bit, row_size) for m, x in held.items()}
        return held

    parts = split_left(left_factor, pieces[:1], span)
    parts, right_factor, left_factor = together((parts, right_factor, left_factor))
    owns = [turn(right_factor, starts[0], chunks[0])]
    owns[0], right_factor, left_factor = together((owns[0], right_factor, left_factor))

    def gathered(parts):
        return [lax.all_gather(part, "col", axis=0, tiled=True) for part in parts]

    lefts = gathered(parts)
    total = jnp.zeros((width_a * width_b, pair_count), jnp.float32)
    rights = [spread({0: owns[0]})]
    for j, calls in enumerate(STAGES):
        moving = j < len(chunks)
        if moving:
            far = swap(owns[j], "row", far_bit, row_size)
        if j == 0:
            owns.append(turn(right_factor, starts[1], chunks[1]))
        if j == 1:
            parts = split_left(left_factor, pieces[1:], span)
            lefts += gathered(parts)
            parts, right_factor = together((parts, right_factor))
            owns += [turn(right_factor, s, n) for s, n in zip(starts[2:], chunks[2:])]
            owns, amplitudes = together((owns, amplitudes))
            amp = jnp.transpose(amplitudes, (1, 0, 2))
        for chosen, js in calls:
            total = add_ladder(
                place, total, amp, starts[js[0]], span,
                [lefts[k] for k in chosen],
                [[rights[i][m] for m in range(row_size)] for i in js],
                [pieces[k] for k in chosen], step_d,
            )
        if moving:
            if j == 0:
                far, total, right_factor, left_factor, amplitudes = together(
                    (far, total, right_factor, left_factor, amplitudes)
                )
            elif j == 1:
                far, total, amp, rights = together((far, total, amp, rights))
            else:
                far, total, owns = together((far, total, owns))
            rights[j] |= spread({far_bit: far})
            if j + 1 < len(chunks):
                rights.append(spread({0: owns[j + 1]}))
    owners = row_size * col_size
    shares = total.T.reshape(owners, pair_count // owners, width_a * width_b)
    return lax.all_to_all(shares, ("row", "col"), 0, 0, tiled=True).sum(axis=0)


STAGES = (
    (),
    (),
    (((0,), (0, 1)),),
    (((0,), (2,)),),
    (((1,), (0, 1, 2)), ((0, 1), (3,))),
    (((0, 1), (4,)), ((2,), (0, 1))),
    (((2,), (2, 3)), ((0, 1, 2), (5,))),
    (((2,), (4,)), ((0, 1, 2), (6,))),
)


def solution(mesh):
    return jax.shard_map(
        functools.partial(on_device, row_size=mesh.shape["row"], col_size=mesh.shape["col"]),
        mesh=mesh,
        in_specs=(
            P(("parts", "col"), None, "row"),
            P("parts", "col", "row"),
            P("row", "col", "parts"),
        ),
        out_specs=P(("parts", "row", "col"), None),
        check_vma=False,
    )
```

```python
import functools
import math

import jax
import jax.numpy as jnp
from jax import lax
from jax.experimental import pallas as pl
from jax.experimental.pallas import tpu as pltpu
from jax.sharding import PartitionSpec as P

CHUNK_SHARES = (1, 4, 3, 2, 2, 2, 2)
PIECES = ((0, 8, 0), (0, 4, 1), (4, 4, 1))


def ladder_kernel(place_ref, total_ref, amp_ref, *refs, pieces, chunk_steps, ranks, first_step, span):
    count_l, count_r = len(pieces), len(chunk_steps) * ranks
    left_refs, right_refs = refs[:count_l], refs[count_l : count_l + count_r]
    out_ref = refs[count_l + count_r]
    rest = refs[count_l + count_r + 1 :]
    left_bufs = rest[:count_l]
    right_buf, amp_buf, integral_ref, left_sem, right_sem, amp_sem, total_sem = rest[count_l:]
    _, _, step_d, width_b, depth = right_buf.shape
    steps = sum(chunk_steps)
    halves = sorted({half for _, _, half in pieces})
    low_c, wide_c = halves[0] * span, len(halves) * span
    step = pl.program_id(0)
    slot = lax.rem(step, 2)
    place = place_ref[0]

    def left_copies(k, a):
        columns = pl.ds(a * span, min(pieces[k][1], 4) * span)
        return [
            pltpu.make_async_copy(
                left_refs[k].at[pl.ds(m * depth, depth), columns],
                left_bufs[k].at[pl.ds(m * depth, depth), columns],
                left_sem.at[k, a // 4, m],
            )
            for m in range(ranks)
        ]

    def total_copy():
        return pltpu.make_async_copy(total_ref, out_ref, total_sem)

    def right_copy(j, offset, to, m):
        source = right_refs[j * ranks + m].at[pl.ds(offset * step_d, step_d)]
        return pltpu.make_async_copy(source, right_buf.at[to, m], right_sem.at[to, m])

    def amp_copy(at, to):
        rows = pl.ds((first_step + at) * step_d, step_d)
        return pltpu.make_async_copy(
            amp_ref.at[rows, pl.ds(low_c, wide_c)], amp_buf.at[to], amp_sem.at[to]
        )

    def fetch_right(at, to):
        begin = 0
        for j, n in enumerate(chunk_steps):

            @pl.when((at >= begin) & (at < begin + n))
            def _():
                for m in range(ranks):
                    right_copy(j, at - begin, to, m).start()

            begin += n

    def fetch_rest():
        total_copy().start()
        amp_copy(0, 0).start()
        if steps > 1:
            fetch_right(1, 1)

    def integrals(to, first):
        row = 0
        for k, (_, count, _) in enumerate(pieces):
            wide = min(count, 4)
            for a in range(0, count, wide):
                if first:
                    for copy in left_copies(k, a):
                        copy.wait()
                    if k == 0 and a == 0:
                        fetch_rest()
                product = None
                for m in range(ranks):
                    start = pl.multiple_of((place ^ m) * depth, depth)
                    term = jnp.dot(
                        right_buf[to, m].reshape(step_d * width_b, depth),
                        left_bufs[k][pl.ds(start, depth), a * span : (a + wide) * span],
                        preferred_element_type=jnp.float32,
                    )
                    product = term if product is None else product + term
                rounded = product.astype(jnp.bfloat16)
                for i in range(wide):
                    for d in range(step_d):
                        integral_ref[to, row : row + width_b, d * span : (d + 1) * span] = rounded[
                            d * width_b : (d + 1) * width_b, i * span : (i + 1) * span
                        ]
                    row += width_b

    def ladder(at):
        row = 0
        for first, count, half in pieces:
            low = halves.index(half) * span
            weights = amp_buf[at, :, low : low + span, :].reshape(step_d * span, amp_buf.shape[3])
            size = count * width_b
            out_ref[first * width_b : first * width_b + size, :] += jnp.dot(
                integral_ref[at, row : row + size, :], weights, preferred_element_type=jnp.float32
            )
            row += size

    @pl.when(step == 0)
    def _():
        for m in range(ranks):
            right_copy(0, 0, 0, m).start()
        for k, (_, count, _) in enumerate(pieces):
            for a in range(0, count, 4):
                for copy in left_copies(k, a):
                    copy.start()

    if steps > 1:

        @pl.when(step > 0)
        def _():
            amp_copy(step, slot).start()

        @pl.when((step > 0) & (step + 1 < steps))
        def _():
            fetch_right(step + 1, 1 - slot)

    for m in range(ranks):
        right_copy(0, 0, slot, m).wait()

    @pl.when(step == 0)
    def _():
        integrals(0, True)
        total_copy().wait()

    if steps > 1:

        @pl.when(step > 0)
        def _():
            amp_copy(0, 1 - slot).wait()
            ladder(1 - slot)
            integrals(slot, False)

    @pl.when(step == steps - 1)
    def _():
        amp_copy(0, slot).wait()
        ladder(slot)


def add_ladder(place, total, amp, first_d, span, lefts, rights, pieces, step_d):
    _, width_b, depth = rights[0][0].shape
    ranks = len(rights[0])
    pair_count = amp.shape[2]
    chunk_steps = tuple(blocks[0].shape[0] // step_d for blocks in rights)
    steps = sum(chunk_steps)
    halves = {half for _, _, half in pieces}
    count_a = sum(count for _, count, _ in pieces)
    columns = count_a * span
    flops = 2 * steps * step_d * width_b * columns * (depth * ranks + pair_count)
    blocks = [block for chunk in rights for block in chunk]
    anywhere = pl.BlockSpec(memory_space=pl.ANY)
    return pl.pallas_call(
        functools.partial(
            ladder_kernel,
            pieces=pieces,
            chunk_steps=chunk_steps,
            ranks=ranks,
            first_step=first_d // step_d,
            span=span,
        ),
        out_shape=jax.ShapeDtypeStruct(total.shape, total.dtype),
        grid_spec=pltpu.PrefetchScalarGridSpec(
            num_scalar_prefetch=1,
            grid=(steps,),
            in_specs=[anywhere] * (2 + len(lefts) + len(blocks)),
            out_specs=pl.BlockSpec(total.shape, lambda s, _: (0, 0)),
            scratch_shapes=[pltpu.VMEM(x.shape, x.dtype) for x in lefts]
            + [
                pltpu.VMEM((2, ranks, step_d, width_b, depth), jnp.bfloat16),
                pltpu.VMEM((2, step_d, span * len(halves), pair_count), jnp.bfloat16),
                pltpu.VMEM((2, count_a * width_b, step_d * span), jnp.bfloat16),
                pltpu.SemaphoreType.DMA((len(lefts), -(-max(n for _, n, _ in pieces) // 4), ranks)),
                pltpu.SemaphoreType.DMA((2, ranks)),
                pltpu.SemaphoreType.DMA((2,)),
                pltpu.SemaphoreType.DMA(()),
            ],
        ),
        input_output_aliases={1: 0},
        compiler_params=pltpu.CompilerParams(vmem_limit_bytes=VMEM_BYTES),
        cost_estimate=pl.CostEstimate(
            flops=flops // 20,
            bytes_accessed=2 * depth * ranks * (columns + steps * step_d * width_b),
            transcendentals=0,
        ),
    )(place, total, amp, *lefts, *blocks)


VMEM_BYTES = 62 * 2**20
SMALL_COST = pl.CostEstimate(flops=0, bytes_accessed=2**16, transcendentals=0)


def turn_kernel(in_ref, out_ref, wide_ref):
    outer, inner, width = in_ref.shape
    for k in range(width // 128):
        lanes = slice(k * 128, (k + 1) * 128)
        wide_ref[k] = in_ref[:, :, lanes].astype(jnp.float32).reshape(outer * inner, 128)
        for i in range(inner):
            out_ref[i, :, lanes] = wide_ref[k, pl.ds(i, outer, stride=inner), :].astype(out_ref.dtype)


def turn(array, start, size):
    outer, _, width = array.shape
    inner = 16
    if start % inner or size % inner or width % 128 or outer % 16:
        return jnp.transpose(array[:, start : start + size], (1, 0, 2))
    block = math.gcd(outer, 64)
    return pl.pallas_call(
        turn_kernel,
        out_shape=jax.ShapeDtypeStruct((size, outer, width), array.dtype),
        grid=(size // inner, outer // block),
        in_specs=[pl.BlockSpec((block, inner, width), lambda i, j: (j, start // inner + i, 0))],
        out_specs=pl.BlockSpec((inner, block, width), lambda i, j: (i, j, 0)),
        scratch_shapes=[pltpu.VMEM((width // 128, block * inner, 128), jnp.float32)],
        compiler_params=pltpu.CompilerParams(vmem_limit_bytes=VMEM_BYTES),
        cost_estimate=SMALL_COST,
    )(array)


def split_kernel(in_ref, *refs, pieces, span):
    wide_ref = refs[-1]
    rows, count_a, _ = in_ref.shape
    wide_ref[...] = in_ref[...].astype(jnp.float32).reshape(rows * count_a, span)
    for (first, count, _), out_ref in zip(pieces, refs):
        for a in range(count):
            picked = wide_ref[pl.ds(first + a, rows, stride=count_a), :]
            out_ref[:, a * span : (a + 1) * span] = picked.astype(out_ref.dtype)


def split_left(array, pieces, span):
    rows, count_a, _ = array.shape
    half = pieces[0][2]
    block = math.gcd(rows, 256)
    return pl.pallas_call(
        functools.partial(split_kernel, pieces=pieces, span=span),
        out_shape=[jax.ShapeDtypeStruct((rows, count * span), array.dtype) for _, count, _ in pieces],
        grid=(rows // block,),
        in_specs=[pl.BlockSpec((block, count_a, span), lambda i: (i, 0, half))],
        out_specs=[pl.BlockSpec((block, count * span), lambda i: (i, 0)) for _, count, _ in pieces],
        scratch_shapes=[pltpu.VMEM((block * count_a, span), jnp.float32)],
        compiler_params=pltpu.CompilerParams(vmem_limit_bytes=VMEM_BYTES),
        cost_estimate=SMALL_COST,
    )(array)


def swap(block, axis, bit, size):
    return lax.ppermute(block, axis, [(i, i ^ bit) for i in range(size)])


def on_device(left_factor, right_factor, amplitudes, *, row_size, col_size):
    width_a = left_factor.shape[1]
    span_c = left_factor.shape[2]
    width_b, span_d, depth = right_factor.shape
    pair_count = amplitudes.shape[2]
    span = span_c // 2
    place = lax.axis_index("row").astype(jnp.int32).reshape(1)

    pieces = [(f * width_a // 8, n * width_a // 8, h) for f, n, h in PIECES]

    chunks = [share * span_d // 16 for share in CHUNK_SHARES]
    starts = [sum(chunks[:j]) for j in range(len(chunks))]
    step_d = math.gcd(16, *chunks)

    together = lax.optimization_barrier
    far_bit = row_size // 2
    near_bits = [1 << k for k in reversed(range(row_size.bit_length() - 2))]

    def spread(held):
        for bit in near_bits:
            held = held | {m ^ bit: swap(x, "row", bit, row_size) for m, x in held.items()}
        return held

    parts = split_left(left_factor, pieces[:1], span)
    parts, right_factor, left_factor = together((parts, right_factor, left_factor))
    owns = [turn(right_factor, starts[0], chunks[0])]
    owns[0], right_factor, left_factor = together((owns[0], right_factor, left_factor))

    def gathered(parts):
        return [lax.all_gather(part, "col", axis=0, tiled=True) for part in parts]

    lefts = gathered(parts)
    total = jnp.zeros((width_a * width_b, pair_count), jnp.float32)
    rights = [spread({0: owns[0]})]
    for j, calls in enumerate(STAGES):
        moving = j < len(chunks)
        if moving:
            far = swap(owns[j], "row", far_bit, row_size)
        if j == 0:
            owns.append(turn(right_factor, starts[1], chunks[1]))
        if j == 1:
            parts = split_left(left_factor, pieces[1:], span)
            lefts += gathered(parts)
            parts, right_factor = together((parts, right_factor))
            owns += [turn(right_factor, s, n) for s, n in zip(starts[2:], chunks[2:])]
            owns, amplitudes = together((owns, amplitudes))
            amp = jnp.transpose(amplitudes, (1, 0, 2))
        for chosen, js in calls:
            total = add_ladder(
                place, total, amp, starts[js[0]], span,
                [lefts[k] for k in chosen],
                [[rights[i][m] for m in range(row_size)] for i in js],
                [pieces[k] for k in chosen], step_d,
            )
        if moving:
            if j == 0:
                far, total, right_factor, left_factor, amplitudes = together(
                    (far, total, right_factor, left_factor, amplitudes)
                )
            elif j == 1:
                far, total, amp, rights = together((far, total, amp, rights))
            else:
                far, total, owns = together((far, total, owns))
            rights[j] |= spread({far_bit: far})
            if j + 1 < len(chunks):
                rights.append(spread({0: owns[j + 1]}))
    owners = row_size * col_size
    shares = total.T.reshape(owners, pair_count // owners, width_a * width_b)
    return lax.all_to_all(shares, ("row", "col"), 0, 0, tiled=True).sum(axis=0)


STAGES = (
    (),
    (),
    (((0,), (0, 1)),),
    (((0,), (2,)),),
    (((1,), (0, 1, 2)), ((0, 1), (3,))),
    (((0, 1), (4,)), ((2,), (0, 1))),
    (((2,), (2, 3)), ((0, 1, 2), (5,))),
    (((2,), (4,)), ((0, 1, 2), (6,))),
)


def solution(mesh):
    return jax.shard_map(
        functools.partial(on_device, row_size=mesh.shape["row"], col_size=mesh.shape["col"]),
        mesh=mesh,
        in_specs=(
            P(("parts", "col"), None, "row"),
            P("parts", "col", "row"),
            P("row", "col", "parts"),
        ),
        out_specs=P(("parts", "row", "col"), None),
        check_vma=False,
    )
```

```python
import functools
import math

import jax
import jax.numpy as jnp
from jax import lax
from jax.experimental import pallas as pl
from jax.experimental.pallas import tpu as pltpu
from jax.sharding import PartitionSpec as P

CHUNK_SHARES = (2, 3, 3, 2, 2, 2, 2)
PIECES = ((0, 8, 0), (0, 4, 1), (4, 4, 1))


def ladder_kernel(place_ref, total_ref, amp_ref, *refs, pieces, chunk_steps, ranks, first_step, span):
    count_l, count_r = len(pieces), len(chunk_steps) * ranks
    left_refs, right_refs = refs[:count_l], refs[count_l : count_l + count_r]
    out_ref = refs[count_l + count_r]
    rest = refs[count_l + count_r + 1 :]
    left_bufs = rest[:count_l]
    right_buf, amp_buf, integral_ref, left_sem, right_sem, amp_sem, total_sem = rest[count_l:]
    _, _, step_d, width_b, depth = right_buf.shape
    steps = sum(chunk_steps)
    halves = sorted({half for _, _, half in pieces})
    low_c, wide_c = halves[0] * span, len(halves) * span
    step = pl.program_id(0)
    slot = lax.rem(step, 2)
    place = place_ref[0]

    def left_copies(k, a):
        columns = pl.ds(a * span, min(pieces[k][1], 4) * span)
        return [
            pltpu.make_async_copy(
                left_refs[k].at[pl.ds(m * depth, depth), columns],
                left_bufs[k].at[pl.ds(m * depth, depth), columns],
                left_sem.at[k, a // 4, m],
            )
            for m in range(ranks)
        ]

    def total_copy():
        return pltpu.make_async_copy(total_ref, out_ref, total_sem)

    def right_copy(j, offset, to, m):
        source = right_refs[j * ranks + m].at[pl.ds(offset * step_d, step_d)]
        return pltpu.make_async_copy(source, right_buf.at[to, m], right_sem.at[to, m])

    def amp_copy(at, to):
        rows = pl.ds((first_step + at) * step_d, step_d)
        return pltpu.make_async_copy(
            amp_ref.at[rows, pl.ds(low_c, wide_c)], amp_buf.at[to], amp_sem.at[to]
        )

    def fetch_right(at, to):
        begin = 0
        for j, n in enumerate(chunk_steps):

            @pl.when((at >= begin) & (at < begin + n))
            def _():
                for m in range(ranks):
                    right_copy(j, at - begin, to, m).start()

            begin += n

    def fetch_rest():
        total_copy().start()
        amp_copy(0, 0).start()
        if steps > 1:
            fetch_right(1, 1)

    def integrals(to, first):
        row = 0
        for k, (_, count, _) in enumerate(pieces):
            wide = min(count, 4)
            for a in range(0, count, wide):
                if first:
                    for copy in left_copies(k, a):
                        copy.wait()
                    if k == 0 and a == 0:
                        fetch_rest()
                product = None
                for m in range(ranks):
                    start = pl.multiple_of((place ^ m) * depth, depth)
                    term = jnp.dot(
                        right_buf[to, m].reshape(step_d * width_b, depth),
                        left_bufs[k][pl.ds(start, depth), a * span : (a + wide) * span],
                        preferred_element_type=jnp.float32,
                    )
                    product = term if product is None else product + term
                rounded = product.astype(jnp.bfloat16)
                for i in range(wide):
                    for d in range(step_d):
                        integral_ref[to, row : row + width_b, d * span : (d + 1) * span] = rounded[
                            d * width_b : (d + 1) * width_b, i * span : (i + 1) * span
                        ]
                    row += width_b

    def ladder(at):
        row = 0
        for first, count, half in pieces:
            low = halves.index(half) * span
            weights = amp_buf[at, :, low : low + span, :].reshape(step_d * span, amp_buf.shape[3])
            size = count * width_b
            out_ref[first * width_b : first * width_b + size, :] += jnp.dot(
                integral_ref[at, row : row + size, :], weights, preferred_element_type=jnp.float32
            )
            row += size

    @pl.when(step == 0)
    def _():
        for m in range(ranks):
            right_copy(0, 0, 0, m).start()
        for k, (_, count, _) in enumerate(pieces):
            for a in range(0, count, 4):
                for copy in left_copies(k, a):
                    copy.start()

    if steps > 1:

        @pl.when(step > 0)
        def _():
            amp_copy(step, slot).start()

        @pl.when((step > 0) & (step + 1 < steps))
        def _():
            fetch_right(step + 1, 1 - slot)

    for m in range(ranks):
        right_copy(0, 0, slot, m).wait()

    @pl.when(step == 0)
    def _():
        integrals(0, True)
        total_copy().wait()

    if steps > 1:

        @pl.when(step > 0)
        def _():
            amp_copy(0, 1 - slot).wait()
            ladder(1 - slot)
            integrals(slot, False)

    @pl.when(step == steps - 1)
    def _():
        amp_copy(0, slot).wait()
        ladder(slot)


def add_ladder(place, total, amp, first_d, span, lefts, rights, pieces, step_d):
    _, width_b, depth = rights[0][0].shape
    ranks = len(rights[0])
    pair_count = amp.shape[2]
    chunk_steps = tuple(blocks[0].shape[0] // step_d for blocks in rights)
    steps = sum(chunk_steps)
    halves = {half for _, _, half in pieces}
    count_a = sum(count for _, count, _ in pieces)
    columns = count_a * span
    flops = 2 * steps * step_d * width_b * columns * (depth * ranks + pair_count)
    blocks = [block for chunk in rights for block in chunk]
    anywhere = pl.BlockSpec(memory_space=pl.ANY)
    return pl.pallas_call(
        functools.partial(
            ladder_kernel,
            pieces=pieces,
            chunk_steps=chunk_steps,
            ranks=ranks,
            first_step=first_d // step_d,
            span=span,
        ),
        out_shape=jax.ShapeDtypeStruct(total.shape, total.dtype),
        grid_spec=pltpu.PrefetchScalarGridSpec(
            num_scalar_prefetch=1,
            grid=(steps,),
            in_specs=[anywhere] * (2 + len(lefts) + len(blocks)),
            out_specs=pl.BlockSpec(total.shape, lambda s, _: (0, 0)),
            scratch_shapes=[pltpu.VMEM(x.shape, x.dtype) for x in lefts]
            + [
                pltpu.VMEM((2, ranks, step_d, width_b, depth), jnp.bfloat16),
                pltpu.VMEM((2, step_d, span * len(halves), pair_count), jnp.bfloat16),
                pltpu.VMEM((2, count_a * width_b, step_d * span), jnp.bfloat16),
                pltpu.SemaphoreType.DMA((len(lefts), -(-max(n for _, n, _ in pieces) // 4), ranks)),
                pltpu.SemaphoreType.DMA((2, ranks)),
                pltpu.SemaphoreType.DMA((2,)),
                pltpu.SemaphoreType.DMA(()),
            ],
        ),
        input_output_aliases={1: 0},
        compiler_params=pltpu.CompilerParams(vmem_limit_bytes=VMEM_BYTES),
        cost_estimate=pl.CostEstimate(
            flops=flops // 20,
            bytes_accessed=2 * depth * ranks * (columns + steps * step_d * width_b),
            transcendentals=0,
        ),
    )(place, total, amp, *lefts, *blocks)


VMEM_BYTES = 62 * 2**20
SMALL_COST = pl.CostEstimate(flops=0, bytes_accessed=2**16, transcendentals=0)


def turn_kernel(in_ref, out_ref, wide_ref):
    outer, inner, width = in_ref.shape
    for k in range(width // 128):
        lanes = slice(k * 128, (k + 1) * 128)
        wide_ref[k] = in_ref[:, :, lanes].astype(jnp.float32).reshape(outer * inner, 128)
        for i in range(inner):
            out_ref[i, :, lanes] = wide_ref[k, pl.ds(i, outer, stride=inner), :].astype(out_ref.dtype)


def turn(array, start, size):
    outer, _, width = array.shape
    inner = 16
    if start % inner or size % inner or width % 128 or outer % 16:
        return jnp.transpose(array[:, start : start + size], (1, 0, 2))
    block = math.gcd(outer, 64)
    return pl.pallas_call(
        turn_kernel,
        out_shape=jax.ShapeDtypeStruct((size, outer, width), array.dtype),
        grid=(size // inner, outer // block),
        in_specs=[pl.BlockSpec((block, inner, width), lambda i, j: (j, start // inner + i, 0))],
        out_specs=pl.BlockSpec((inner, block, width), lambda i, j: (i, j, 0)),
        scratch_shapes=[pltpu.VMEM((width // 128, block * inner, 128), jnp.float32)],
        compiler_params=pltpu.CompilerParams(vmem_limit_bytes=VMEM_BYTES),
        cost_estimate=SMALL_COST,
    )(array)


def split_kernel(in_ref, *refs, pieces, span):
    wide_ref = refs[-1]
    rows, count_a, _ = in_ref.shape
    wide_ref[...] = in_ref[...].astype(jnp.float32).reshape(rows * count_a, span)
    for (first, count, _), out_ref in zip(pieces, refs):
        for a in range(count):
            picked = wide_ref[pl.ds(first + a, rows, stride=count_a), :]
            out_ref[:, a * span : (a + 1) * span] = picked.astype(out_ref.dtype)


def split_left(array, pieces, span):
    rows, count_a, _ = array.shape
    half = pieces[0][2]
    block = math.gcd(rows, 256)
    return pl.pallas_call(
        functools.partial(split_kernel, pieces=pieces, span=span),
        out_shape=[jax.ShapeDtypeStruct((rows, count * span), array.dtype) for _, count, _ in pieces],
        grid=(rows // block,),
        in_specs=[pl.BlockSpec((block, count_a, span), lambda i: (i, 0, half))],
        out_specs=[pl.BlockSpec((block, count * span), lambda i: (i, 0)) for _, count, _ in pieces],
        scratch_shapes=[pltpu.VMEM((block * count_a, span), jnp.float32)],
        compiler_params=pltpu.CompilerParams(vmem_limit_bytes=VMEM_BYTES),
        cost_estimate=SMALL_COST,
    )(array)


def swap(block, axis, bit, size):
    return lax.ppermute(block, axis, [(i, i ^ bit) for i in range(size)])


def on_device(left_factor, right_factor, amplitudes, *, row_size, col_size):
    width_a = left_factor.shape[1]
    span_c = left_factor.shape[2]
    width_b, span_d, depth = right_factor.shape
    pair_count = amplitudes.shape[2]
    span = span_c // 2
    place = lax.axis_index("row").astype(jnp.int32).reshape(1)

    pieces = [(f * width_a // 8, n * width_a // 8, h) for f, n, h in PIECES]

    chunks = [share * span_d // 16 for share in CHUNK_SHARES]
    starts = [sum(chunks[:j]) for j in range(len(chunks))]
    step_d = math.gcd(16, *chunks)

    together = lax.optimization_barrier
    far_bit = row_size // 2
    near_bits = [1 << k for k in reversed(range(row_size.bit_length() - 2))]

    def spread(held):
        for bit in near_bits:
            held = held | {m ^ bit: swap(x, "row", bit, row_size) for m, x in held.items()}
        return held

    parts = split_left(left_factor, pieces[:1], span)
    parts, right_factor, left_factor = together((parts, right_factor, left_factor))
    owns = [turn(right_factor, starts[0], chunks[0])]
    owns[0], right_factor, left_factor = together((owns[0], right_factor, left_factor))

    def gathered(parts):
        return [lax.all_gather(part, "col", axis=0, tiled=True) for part in parts]

    lefts = gathered(parts)
    total = jnp.zeros((width_a * width_b, pair_count), jnp.float32)
    rights = [spread({0: owns[0]})]
    for j, calls in enumerate(STAGES):
        moving = j < len(chunks)
        if moving:
            far = swap(owns[j], "row", far_bit, row_size)
        if j == 0:
            owns.append(turn(right_factor, starts[1], chunks[1]))
        if j == 1:
            parts = split_left(left_factor, pieces[1:], span)
            lefts += gathered(parts)
            parts, right_factor = together((parts, right_factor))
            owns += [turn(right_factor, s, n) for s, n in zip(starts[2:], chunks[2:])]
            owns, amplitudes = together((owns, amplitudes))
            amp = jnp.transpose(amplitudes, (1, 0, 2))
        for chosen, js in calls:
            total = add_ladder(
                place, total, amp, starts[js[0]], span,
                [lefts[k] for k in chosen],
                [[rights[i][m] for m in range(row_size)] for i in js],
                [pieces[k] for k in chosen], step_d,
            )
        if moving:
            if j == 0:
                far, total, right_factor, left_factor, amplitudes = together(
                    (far, total, right_factor, left_factor, amplitudes)
                )
            elif j == 1:
                far, total, amp, rights = together((far, total, amp, rights))
            else:
                far, total, owns = together((far, total, owns))
            rights[j] |= spread({far_bit: far})
            if j + 1 < len(chunks):
                rights.append(spread({0: owns[j + 1]}))
    owners = row_size * col_size
    shares = total.T.reshape(owners, pair_count // owners, width_a * width_b)
    return lax.all_to_all(shares, ("row", "col"), 0, 0, tiled=True).sum(axis=0)


STAGES = (
    (),
    (),
    (((0,), (0, 1)),),
    (((0,), (2,)),),
    (((1,), (0, 1)), ((0, 1), (3,))),
    (((1,), (2,)), ((0, 1), (4,)), ((2,), (0, 1))),
    (((2,), (2, 3)), ((0, 1, 2), (5,))),
    (((2,), (4,)), ((0, 1, 2), (6,))),
)


def solution(mesh):
    return jax.shard_map(
        functools.partial(on_device, row_size=mesh.shape["row"], col_size=mesh.shape["col"]),
        mesh=mesh,
        in_specs=(
            P(("parts", "col"), None, "row"),
            P("parts", "col", "row"),
            P("row", "col", "parts"),
        ),
        out_specs=P(("parts", "row", "col"), None),
        check_vma=False,
    )
```
